256 devices in a mesh: pts: 16 (over x, y_lo, core), lst: 16 (over z, y_hi).
Axes of the slice: x: 4, y: 4 (y_hi: 2, y_lo: 2; y = y_hi * 2 + y_lo), z: 8, core: 2. Of those that a mesh axis runs over, the one named last changes fastest.
Arguments:
- tower_out: bfloat16 [32768, 1024], P('pts', 'lst'), may hold values from -6 to 6
- projection: bfloat16 [1024, 256], P('lst'), may hold values from -1 to 1
- centroids: bfloat16 [16384, 256], P('lst'), may hold values from -6 to 6
Outputs:
- new_centroids: float32 [16384, 256], P(('lst', 'pts'))
- row_log: float32 [32768], P('pts')
The draws below stay inside these ranges and needn't reach their ends.
All inputs are finite; a program needn't handle non-finite values.
Results may differ from the reference program's by a relative error of at most 0.0045.
Values may be sent and summed in bfloat16 or wider, within the bound.
No kernel may reach another device: no remote copies, remote signals or barrier semaphores. Data moves between devices by JAX's collectives and lax.ppermute only.
A program may use at most 64 MiB of HBM per device.

```python
import math
import jax
import jax.numpy as jnp
from jax import lax

DIN = 1024
DP = 256
KC = 16384
ITERS = 3
NPTS = 32768


strength = 0.35


planted = 1.0


def plus_minus(seeded, total_count):
    return (jax.random.randint(seeded, (total_count,), 0, 2) * 2 - 1).astype(jnp.float32)


def tower_axis(key):
    return plus_minus(jax.random.fold_in(jax.random.fold_in(key, 101), 1), DIN)


def list_axis(key):
    return plus_minus(jax.random.fold_in(jax.random.fold_in(key, 101), 2), DP)


def group_signs(seeded, total_count, lowest, highest):
    border = jax.random.randint(seeded, (), lowest, highest)
    return jnp.where(jnp.arange(total_count) < border, 1.0, -1.0).astype(jnp.float32)


def draw_tower_out(key, part):
    tower_dir = tower_axis(key)
    point_sign = group_signs(jax.random.fold_in(key, 12), NPTS, 65 * NPTS // 100, 80 * NPTS // 100 + 1)
    jitter = jnp.clip(jax.random.normal(jax.random.fold_in(key, 11), (NPTS, DIN), jnp.float32), -5.5, 5.5)
    values = jitter + strength * point_sign[:, None] * tower_dir[None, :]
    return values.astype(jnp.bfloat16)


def draw_projection(key, part):
    tower_dir = tower_axis(key)
    list_dir = list_axis(key)
    dense = jnp.clip(jax.random.normal(jax.random.fold_in(key, 21), (DIN, DP), jnp.float32), -6.0, 6.0)
    values = dense * (1.0 / math.sqrt(DIN)) + planted / DIN * tower_dir[:, None] * list_dir[None, :]
    return values.astype(jnp.bfloat16)


def draw_centroids(key, part):
    list_dir = list_axis(key)
    list_sign = group_signs(jax.random.fold_in(key, 32), KC, 20 * KC // 100, 35 * KC // 100 + 1)
    jitter = jnp.clip(jax.random.normal(jax.random.fold_in(key, 31), (KC, DP), jnp.float32), -5.5, 5.5)
    values = jitter + strength * list_sign[:, None] * list_dir[None, :]
    return values.astype(jnp.bfloat16)


def setup_inputs(seed: int = 0) -> dict:
    key_list = jax.random.split(jax.random.key(seed), 4)
    tower_out = draw_tower_out(jax.random.fold_in(key_list[3], 71), 0)
    projection = draw_projection(jax.random.fold_in(key_list[3], 71), 0)
    centroids = draw_centroids(jax.random.fold_in(key_list[3], 71), 0)
    return dict(tower_out=tower_out, projection=projection, centroids=centroids)


temper = 0.05

def rms_norm(values):
    return values * lax.rsqrt(lax.optimization_barrier(jnp.mean(values * values, axis=-1, keepdims=True)) + 1e-06)

def energy(zblock, unit_lists):
    scores = lax.dot_general(zblock, unit_lists, (((1,), (1,)), ((), ())), preferred_element_type=jnp.float32)
    return jnp.exp(scores / (DP * temper) - 1.0 / temper)

def reference(tower_out, projection, centroids):
    hidden = jnp.dot(tower_out, projection, preferred_element_type=jnp.float32)
    normed = rms_norm(hidden).astype(jnp.bfloat16)
    unit_lists = rms_norm(centroids.astype(jnp.float32)).astype(jnp.bfloat16)
    block_rows = min(512, NPTS)
    block_count = NPTS // block_rows
    blocks = normed.reshape(block_count, block_rows, DP)
    balance = NPTS / KC
    row_scale = jnp.ones((NPTS,), jnp.float32)
    col_scale = jnp.ones((KC,), jnp.float32)
    for sweep in range(ITERS):

        def column_step(running, inputs):
            zblock, scale_blk = inputs
            return (running + lax.optimization_barrier(jnp.sum(energy(zblock, unit_lists) * scale_blk[:, None], axis=0)), None)
        column_sum = lax.scan(column_step, jnp.zeros((KC,), jnp.float32), (blocks, row_scale.reshape(block_count, block_rows)))[0]
        col_scale = balance / column_sum

        def row_step(zblock, scales=col_scale):
            return lax.optimization_barrier(jnp.sum(energy(zblock, unit_lists) * scales[None, :], axis=1))
        row_sum = lax.map(row_step, blocks).reshape(NPTS)
        row_scale = 1.0 / row_sum

    def update_step(running, inputs):
        zblock, scale_blk = inputs
        weights = (scale_blk[:, None] * energy(zblock, unit_lists) * col_scale[None, :]).astype(jnp.bfloat16)
        sums_part = lax.dot_general(weights, zblock, (((0,), (0,)), ((), ())), preferred_element_type=jnp.float32)
        return (running + sums_part, None)
    list_sums = lax.scan(update_step, jnp.zeros((KC, DP), jnp.float32), (blocks, row_scale.reshape(block_count, block_rows)))[0]
    return (rms_norm(list_sums), jnp.log(row_scale))
```

```python
import jax
import jax.numpy as jnp
from jax import lax
from jax.sharding import Mesh, PartitionSpec as P

DP = 256
ITERS = 3
ROWS = 128

temper = 0.05
SWAP = [(0, 1), (1, 0)]
PLANE = ("x", "yl", "c", "yh")
CHIPS = ("yh", "x", "yl")
bf16 = jnp.bfloat16
f32 = jnp.float32


def rms_norm(values):
    return values * lax.rsqrt(jnp.mean(values * values, axis=-1, keepdims=True) + 1e-06)


def energy(points, unit_lists):
    scores = lax.dot_general(
        points, unit_lists, (((1,), (1,)), ((), ())), preferred_element_type=f32
    )
    return jnp.exp(scores / (DP * temper) - 1.0 / temper)


def gather_all(values, axis, size):
    return lax.all_to_all(jnp.broadcast_to(values[None], (size,) + values.shape), axis, 0, 0)


def total(local, axis, size):
    parts = gather_all(local.reshape(-1, 128), axis, size)
    return jnp.sum(parts, axis=0).reshape(local.shape)


def on_device(tower_out, projection, centroids):
    half = lax.axis_index("yh")
    balance = 2.0
    tower = tower_out.T.reshape(64, 8, 2, ROWS)
    kept = jnp.where(half == 0, tower[:, :, 0], tower[:, :, 1]).reshape(64, 8 * ROWS)
    given = jnp.where(half == 0, tower[:, :, 1], tower[:, :, 0]).reshape(64, 8 * ROWS)
    taken = lax.ppermute(given, "yh", SWAP)
    taken_projection = lax.ppermute(projection, "yh", SWAP)
    taken_centroids = lax.ppermute(centroids, "yh", SWAP)

    contract = (((0,), (0,)), ((), ()))
    partial = lax.dot_general(kept, projection, contract, preferred_element_type=f32)
    partial += lax.dot_general(taken, taken_projection, contract, preferred_element_type=f32)
    partial = partial.astype(bf16).reshape(8, ROWS, DP)
    shares = lax.all_to_all(partial, "z", 0, 0)
    hidden = jnp.sum(shares.astype(f32), axis=0)
    own = rms_norm(hidden).astype(bf16)
    normed = gather_all(own, "z", 8).reshape(8 * ROWS, DP)

    low = jnp.where(half == 0, centroids, taken_centroids)
    high = jnp.where(half == 0, taken_centroids, centroids)
    unit_lists = rms_norm(jnp.concatenate([low, high]).astype(f32)).astype(bf16)

    row_scale = jnp.ones((8 * ROWS,), f32)
    for sweep in range(ITERS):
        column_local = jnp.sum(energy(normed, unit_lists) * row_scale[:, None], axis=0)
        col_scale = balance / total(column_local, PLANE, 32)
        row_local = jnp.sum(energy(normed, unit_lists) * col_scale[None, :], axis=1)
        row_scale = 1.0 / total(row_local, "z", 8)

    row_log = jnp.log(row_scale).reshape(8, ROWS)
    taken_log = lax.ppermute(row_log, "yh", SWAP)
    low_log = jnp.where(half == 0, row_log, taken_log)
    high_log = jnp.where(half == 0, taken_log, row_log)
    row_log = jnp.stack([low_log, high_log], axis=1).reshape(16 * ROWS)

    weights = row_scale[:, None] * energy(normed, unit_lists) * col_scale[None, :]
    list_sums = lax.dot_general(
        weights.astype(bf16), normed, (((0,), (0,)), ((), ())), preferred_element_type=f32
    )
    by_core = list_sums.reshape(16, 2, 64, DP)
    core = lax.axis_index("c")
    mine = jnp.where(core == 0, by_core[:, 0], by_core[:, 1])
    theirs = jnp.where(core == 0, by_core[:, 1], by_core[:, 0])
    mine += lax.ppermute(theirs, "c", SWAP)
    owned = jnp.sum(lax.all_to_all(mine.astype(bf16), CHIPS, 0, 0).astype(f32), axis=0)
    return (rms_norm(owned), row_log)


def solution(mesh):
    fine = Mesh(mesh.devices.reshape(4, 2, 2, 8, 2), ("x", "yl", "c", "z", "yh"))
    pts, lst = ("x", "yl", "c"), ("z", "yh")
    return jax.shard_map(
        on_device,
        mesh=fine,
        in_specs=(P(pts, lst), P(lst, None), P(lst, None)),
        out_specs=(P(lst + pts, None), P(pts)),
        check_vma=False,
    )
```

```python
import jax
import jax.numpy as jnp
from jax import lax
from jax.experimental import pallas as pl
from jax.experimental.pallas import tpu as pltpu
from jax.sharding import Mesh, PartitionSpec as P

DP = 256
ITERS = 3
ROWS = 128

temper = 0.05
SWAP = [(0, 1), (1, 0)]
PLANE = ("x", "yl", "c", "yh")
CHIPS = ("yh", "x", "yl")
bf16 = jnp.bfloat16
f32 = jnp.float32


def rms_norm(values):
    return values * lax.rsqrt(jnp.mean(values * values, axis=-1, keepdims=True) + 1e-06)


VMEM = pltpu.VMEM
LIMIT = pltpu.CompilerParams(vmem_limit_bytes=40 * 2**20)


def whole(count):
    return [pl.BlockSpec(memory_space=VMEM)] * count


def stay(array):
    return pltpu.with_memory_space_constraint(array, VMEM)


def split_rows(row):
    high = row.astype(bf16).astype(f32)
    index = lax.broadcasted_iota(jnp.int32, (16, row.shape[1]), 0)
    lhs = jnp.where(index == 0, high, jnp.where(index == 1, row - high, 0.0))
    return lhs.astype(bf16)


def to_lanes(tile):
    return jnp.concatenate([tile[k : k + 1] for k in range(tile.shape[0])], axis=1)


def to_tile(rows):
    line = rows[0:1] + rows[1:2]
    return jnp.concatenate(
        [line[:, 128 * k : 128 * (k + 1)] for k in range(line.shape[1] // 128)], axis=0
    )


def add_parts(ref):
    tile = ref[0]
    for k in range(1, ref.shape[0]):
        tile += ref[k]
    return tile


def column_sums(row_scale, energy_t):
    return to_tile(
        lax.dot_general(
            split_rows(to_lanes(row_scale)),
            energy_t,
            (((1,), (1,)), ((), ())),
            preferred_element_type=f32,
        )
    )


def energy_kernel(points_ref, lists_ref, energy_ref, column_ref):
    points = points_ref[...].reshape(8 * ROWS, DP)
    for k in range(8):
        rows = pl.ds(256 * k, 256)
        scores = lax.dot_general(
            lists_ref[rows, :], points, (((1,), (1,)), ((), ())), preferred_element_type=f32
        )
        energy_ref[rows, :] = jnp.exp(scores * (1.0 / (DP * temper)) - 1.0 / temper).astype(bf16)
    local = column_sums(jnp.ones((8, 128), f32), energy_ref[...])
    column_ref[...] = jnp.broadcast_to(local[None], column_ref.shape)


def row_kernel(parts_ref, energy_ref, row_ref):
    col_scale = 2.0 / add_parts(parts_ref)
    local = to_tile(
        jnp.dot(split_rows(to_lanes(col_scale)), energy_ref[...], preferred_element_type=f32)
    )
    row_ref[...] = jnp.broadcast_to(local[None], row_ref.shape)


def column_kernel(parts_ref, energy_ref, column_ref):
    local = column_sums(1.0 / add_parts(parts_ref), energy_ref[...])
    column_ref[...] = jnp.broadcast_to(local[None], column_ref.shape)


def down_lanes(row):
    return jnp.transpose(jnp.broadcast_to(row, (128, 128)))


def update_kernel(core_ref, rows_ref, columns_ref, energy_ref, points_ref, mine_ref, other_ref):
    core = core_ref[0]
    row_scale = 1.0 / add_parts(rows_ref)
    col_scale = 2.0 / add_parts(columns_ref)
    scaled = []
    for k in range(8):
        factor = down_lanes(row_scale[k : k + 1])
        block = points_ref[k].astype(f32)
        scaled.append((block * jnp.concatenate([factor, factor], axis=1)).astype(bf16))
    scaled = jnp.concatenate(scaled, axis=0)
    for k in range(16):
        factor = down_lanes(col_scale[k : k + 1])
        sums = jnp.dot(
            energy_ref[pl.ds(128 * k, 128), :], scaled, preferred_element_type=f32
        ) * jnp.concatenate([factor, factor], axis=1)
        mine_ref[k] = jnp.where(core == 0, sums[:64], sums[64:])
        other_ref[k] = jnp.where(core == 0, sums[64:], sums[:64])


def parts_shape(count, rows):
    return jax.ShapeDtypeStruct((count, rows, 128), f32)


def gather_all(values, axis, size):
    return lax.all_to_all(jnp.broadcast_to(values[None], (size,) + values.shape), axis, 0, 0)


def on_device(tower_out, projection, centroids):
    half = lax.axis_index("yh")
    tower = tower_out.T.reshape(64, 8, 2, ROWS)
    kept = jnp.where(half == 0, tower[:, :, 0], tower[:, :, 1]).reshape(64, 8 * ROWS)
    given = jnp.where(half == 0, tower[:, :, 1], tower[:, :, 0]).reshape(64, 8 * ROWS)
    taken = lax.ppermute(given, "yh", SWAP)
    taken_projection = lax.ppermute(projection, "yh", SWAP)
    taken_centroids = lax.ppermute(centroids, "yh", SWAP)

    contract = (((0,), (0,)), ((), ()))
    partial = lax.dot_general(kept, projection, contract, preferred_element_type=f32)
    partial += lax.dot_general(taken, taken_projection, contract, preferred_element_type=f32)
    partial = partial.astype(bf16).reshape(8, ROWS, DP)
    shares = lax.all_to_all(partial, "z", 0, 0)
    hidden = jnp.sum(shares.astype(f32), axis=0)
    own = rms_norm(hidden).astype(bf16)
    points = gather_all(own, "z", 8)

    low = jnp.where(half == 0, centroids, taken_centroids)
    high = jnp.where(half == 0, taken_centroids, centroids)
    unit_lists = rms_norm(jnp.concatenate([low, high]).astype(f32)).astype(bf16)

    energy, columns = pl.pallas_call(
        energy_kernel,
        out_shape=(VMEM((2048, 1024), bf16), parts_shape(32, 16)),
        in_specs=whole(2),
        out_specs=whole(2),
        compiler_params=LIMIT,
        name="energy",
    )(points, unit_lists)
    for sweep in range(ITERS):
        columns = lax.all_to_all(columns, PLANE, 0, 0)
        rows = pl.pallas_call(
            row_kernel,
            out_shape=parts_shape(8, 8),
            in_specs=whole(2),
            out_specs=whole(1)[0],
            compiler_params=LIMIT,
            name="row_sums",
        )(columns, stay(energy))
        rows = lax.all_to_all(rows, "z", 0, 0)
        if sweep < ITERS - 1:
            columns = pl.pallas_call(
                column_kernel,
                out_shape=parts_shape(32, 16),
                in_specs=whole(2),
                out_specs=whole(1)[0],
                compiler_params=LIMIT,
                name="column_sums",
            )(rows, stay(energy))

    row_log = jnp.log(1.0 / jnp.sum(rows, axis=0))
    taken_log = lax.ppermute(row_log, "yh", SWAP)
    mine, other = pl.pallas_call(
        update_kernel,
        out_shape=(jax.ShapeDtypeStruct((16, 64, DP), f32),) * 2,
        in_specs=[pl.BlockSpec(memory_space=pltpu.SMEM)] + whole(4),
        out_specs=whole(2),
        compiler_params=LIMIT,
        name="update",
    )(lax.axis_index("c").reshape(1), rows, columns, stay(energy), points)
    mine += lax.ppermute(other, "c", SWAP)
    owned = jnp.sum(lax.all_to_all(mine.astype(bf16), CHIPS, 0, 0).astype(f32), axis=0)

    low_log = jnp.where(half == 0, row_log, taken_log)
    high_log = jnp.where(half == 0, taken_log, row_log)
    row_log = jnp.stack([low_log, high_log], axis=1).reshape(16 * ROWS)
    return (rms_norm(owned), row_log)


def solution(mesh):
    fine = Mesh(mesh.devices.reshape(4, 2, 2, 8, 2), ("x", "yl", "c", "z", "yh"))
    pts, lst = ("x", "yl", "c"), ("z", "yh")
    return jax.shard_map(
        on_device,
        mesh=fine,
        in_specs=(P(pts, lst), P(lst, None), P(lst, None)),
        out_specs=(P(lst + pts, None), P(pts)),
        check_vma=False,
    )
```

```python
import jax
import jax.numpy as jnp
from jax import lax
from jax.experimental import pallas as pl
from jax.experimental.pallas import tpu as pltpu
from jax.sharding import Mesh, PartitionSpec as P

DP = 256
ITERS = 3
ROWS = 128

temper = 0.05
SWAP = [(0, 1), (1, 0)]
PLANE = ("x", "yl", "c", "yh")
CHIPS = ("yh", "x", "yl")
bf16 = jnp.bfloat16
f32 = jnp.float32


def rms_norm(values):
    return values * lax.rsqrt(jnp.mean(values * values, axis=-1, keepdims=True) + 1e-06)


VMEM = pltpu.VMEM
LIMIT = pltpu.CompilerParams(vmem_limit_bytes=40 * 2**20)


def whole(count):
    return [pl.BlockSpec(memory_space=VMEM)] * count


def stay(array):
    return pltpu.with_memory_space_constraint(array, VMEM)


def split_rows(row):
    high = row.astype(bf16).astype(f32)
    index = lax.broadcasted_iota(jnp.int32, (16, row.shape[1]), 0)
    lhs = jnp.where(index == 0, high, jnp.where(index == 1, row - high, 0.0))
    return lhs.astype(bf16)


def to_lanes(tile):
    return jnp.concatenate([tile[k : k + 1] for k in range(tile.shape[0])], axis=1)


def to_tile(rows):
    line = rows[0:1] + rows[1:2]
    return jnp.concatenate(
        [line[:, 128 * k : 128 * (k + 1)] for k in range(line.shape[1] // 128)], axis=0
    )


def add_parts(ref):
    tile = ref[0].astype(f32)
    for k in range(1, ref.shape[0]):
        tile += ref[k].astype(f32)
    return tile


def column_sums(row_scale, energy_t):
    return to_tile(
        lax.dot_general(
            split_rows(to_lanes(row_scale)),
            energy_t,
            (((1,), (1,)), ((), ())),
            preferred_element_type=f32,
        )
    )


def hidden_kernel(core_ref, parts_ref, columns_ref, out_ref):
    core = core_ref[0]
    contract = (((0,), (0,)), ((), ()))
    tower = parts_ref[:, :64, :].reshape(1024, ROWS)
    kept = parts_ref[:, 64:, :].reshape(1024, 128)
    taken = columns_ref[...].reshape(1024, 128)
    low = jnp.where(core == 0, kept, taken)
    high = jnp.where(core == 0, taken, kept)
    hidden = lax.dot_general(
        tower, jnp.concatenate([low, high], axis=1), contract, preferred_element_type=f32
    )
    out_ref[...] = jnp.broadcast_to(rms_norm(hidden).astype(bf16)[None], out_ref.shape)


def finish_kernel(parts_ref, out_ref):
    sums = parts_ref[0].astype(f32)
    for k in range(1, 16):
        sums += parts_ref[k].astype(f32)
    out_ref[...] = rms_norm(sums)


def energy_kernel(points_ref, lists_ref, energy_ref, column_ref):
    points = points_ref[...].reshape(8 * ROWS, DP)
    for k in range(8):
        rows = pl.ds(256 * k, 256)
        scores = lax.dot_general(
            lists_ref[rows, :], points, (((1,), (1,)), ((), ())), preferred_element_type=f32
        )
        energy_ref[rows, :] = jnp.exp(scores * (1.0 / (DP * temper)) - 1.0 / temper).astype(bf16)
    local = column_sums(jnp.ones((8, 128), f32), energy_ref[...])
    column_ref[...] = jnp.broadcast_to(local.astype(bf16)[None], column_ref.shape)


def row_kernel(parts_ref, energy_ref, row_ref):
    col_scale = 2.0 / add_parts(parts_ref)
    local = to_tile(
        jnp.dot(split_rows(to_lanes(col_scale)), energy_ref[...], preferred_element_type=f32)
    )
    row_ref[...] = jnp.broadcast_to(local[None], row_ref.shape)


def column_kernel(parts_ref, energy_ref, column_ref):
    local = column_sums(1.0 / add_parts(parts_ref), energy_ref[...])
    column_ref[...] = jnp.broadcast_to(local.astype(bf16)[None], column_ref.shape)


def down_lanes(row):
    return jnp.transpose(jnp.broadcast_to(row, (128, 128)))


def update_kernel(core_ref, rows_ref, columns_ref, energy_ref, points_ref, mine_ref, other_ref, log_ref):
    core = core_ref[0]
    row_scale = 1.0 / add_parts(rows_ref)
    log_ref[...] = jnp.log(row_scale)
    col_scale = 2.0 / add_parts(columns_ref)
    scaled = []
    for k in range(8):
        factor = down_lanes(row_scale[k : k + 1])
        block = points_ref[k].astype(f32)
        scaled.append((block * jnp.concatenate([factor, factor], axis=1)).astype(bf16))
    scaled = jnp.concatenate(scaled, axis=0)
    for k in range(16):
        factor = down_lanes(col_scale[k : k + 1])
        sums = jnp.dot(
            energy_ref[pl.ds(128 * k, 128), :], scaled, preferred_element_type=f32
        ) * jnp.concatenate([factor, factor], axis=1)
        mine_ref[k] = jnp.where(core == 0, sums[:64], sums[64:])
        other_ref[k] = jnp.where(core == 0, sums[64:], sums[:64]).astype(bf16)


def parts_shape(count, rows, dtype):
    return jax.ShapeDtypeStruct((count, rows, 128), dtype)


def on_device(tower_out, projection, centroids):
    half = lax.axis_index("yh")
    core = lax.axis_index("c")
    core_index = core.reshape(1)
    tower = tower_out.T.reshape(64, 16, ROWS).transpose(1, 0, 2)
    columns = jnp.where(core == 0, projection[:, :128], projection[:, 128:])
    message = jnp.concatenate([tower, jnp.broadcast_to(columns[None], (16, 64, 128))], axis=1)
    parts = lax.all_to_all(message, ("z", "yh"), 0, 0)
    taken_columns = lax.ppermute(parts[:, 64:], "c", SWAP)
    spread = pl.pallas_call(
        hidden_kernel,
        out_shape=jax.ShapeDtypeStruct((8, ROWS, DP), bf16),
        in_specs=[pl.BlockSpec(memory_space=pltpu.SMEM)] + whole(2),
        out_specs=whole(1)[0],
        compiler_params=LIMIT,
        name="hidden",
    )(core_index, parts, taken_columns)
    points = lax.all_to_all(spread, "z", 0, 0)

    taken_centroids = lax.ppermute(centroids, "yh", SWAP)
    low = jnp.where(half == 0, centroids, taken_centroids)
    high = jnp.where(half == 0, taken_centroids, centroids)
    unit_lists = rms_norm(jnp.concatenate([low, high]).astype(f32)).astype(bf16)

    energy, columns = pl.pallas_call(
        energy_kernel,
        out_shape=(VMEM((2048, 1024), bf16), parts_shape(32, 16, bf16)),
        in_specs=whole(2),
        out_specs=whole(2),
        compiler_params=LIMIT,
        name="energy",
    )(points, unit_lists)
    for sweep in range(ITERS):
        columns = lax.all_to_all(columns, PLANE, 0, 0)
        rows = pl.pallas_call(
            row_kernel,
            out_shape=parts_shape(8, 8, f32),
            in_specs=whole(2),
            out_specs=whole(1)[0],
            compiler_params=LIMIT,
            name="row_sums",
        )(columns, stay(energy))
        rows = lax.all_to_all(rows, "z", 0, 0)
        if sweep < ITERS - 1:
            columns = pl.pallas_call(
                column_kernel,
                out_shape=parts_shape(32, 16, bf16),
                in_specs=whole(2),
                out_specs=whole(1)[0],
                compiler_params=LIMIT,
                name="column_sums",
            )(rows, stay(energy))

    mine, other, row_log = pl.pallas_call(
        update_kernel,
        out_shape=(
            jax.ShapeDtypeStruct((16, 64, DP), f32),
            jax.ShapeDtypeStruct((16, 64, DP), bf16),
            jax.ShapeDtypeStruct((8, 128), f32),
        ),
        in_specs=[pl.BlockSpec(memory_space=pltpu.SMEM)] + whole(4),
        out_specs=whole(3),
        compiler_params=LIMIT,
        name="update",
    )(core_index, rows, columns, stay(energy), points)
    mine += lax.ppermute(other, "c", SWAP).astype(f32)
    owned = lax.all_to_all(mine.astype(bf16), CHIPS, 0, 0)
    refreshed = pl.pallas_call(
        finish_kernel,
        out_shape=jax.ShapeDtypeStruct((64, DP), f32),
        in_specs=whole(1),
        out_specs=whole(1)[0],
        compiler_params=LIMIT,
        name="finish",
    )(owned)

    taken_log = lax.ppermute(row_log, "yh", SWAP)
    low_log = jnp.where(half == 0, row_log, taken_log)
    high_log = jnp.where(half == 0, taken_log, row_log)
    row_log = jnp.stack([low_log, high_log], axis=1).reshape(16 * ROWS)
    return (refreshed, row_log)


def solution(mesh):
    fine = Mesh(mesh.devices.reshape(4, 2, 2, 8, 2), ("x", "yl", "c", "z", "yh"))
    pts, lst = ("x", "yl", "c"), ("z", "yh")
    return jax.shard_map(
        on_device,
        mesh=fine,
        in_specs=(P(pts, lst), P(lst, None), P(lst, None)),
        out_specs=(P(lst + pts, None), P(pts)),
        check_vma=False,
    )
```

```python
import math

import jax
import jax.numpy as jnp
from jax import lax
from jax.experimental import pallas as pl
from jax.experimental.pallas import tpu as pltpu
from jax.sharding import Mesh, PartitionSpec as P

DP = 256
ITERS = 3
ROWS = 128

temper = 0.05
SLOPE = math.log2(math.e) / (DP * temper)
OFFSET = math.log2(math.e) / temper
SWAP = [(0, 1), (1, 0)]
CHIPS = ("yh", "x", "yl")
LISTS = ("z", "c")
bf16 = jnp.bfloat16
f32 = jnp.float32
VMEM = pltpu.VMEM
SCALAR = pl.BlockSpec(memory_space=pltpu.SMEM)
LIMIT = pltpu.CompilerParams(vmem_limit_bytes=40 * 2**20)
COST = pl.CostEstimate(flops=2**29, bytes_accessed=2**22, transcendentals=2**20)


def whole(count):
    return [pl.BlockSpec(memory_space=VMEM)] * count


def stay(array):
    return pltpu.with_memory_space_constraint(array, VMEM)


def far(array):
    return pltpu.with_memory_space_constraint(array, pltpu.HBM)


def call(kernel, out_shape, name, scalars, count, scratch=(), cost=None):
    single = not isinstance(out_shape, tuple)
    return pl.pallas_call(
        kernel,
        out_shape=out_shape,
        in_specs=[SCALAR] * scalars + whole(count),
        out_specs=whole(1)[0] if single else whole(len(out_shape)),
        scratch_shapes=scratch,
        compiler_params=LIMIT,
        cost_estimate=cost,
        name=name,
    )


def rms_norm(values):
    return values * lax.rsqrt(jnp.mean(values * values, axis=-1, keepdims=True) + 1e-06)


def split_rows(row):
    high = row.astype(bf16).astype(f32)
    index = lax.broadcasted_iota(jnp.int32, (16, row.shape[1]), 0)
    lhs = jnp.where(index == 0, high, jnp.where(index == 1, row - high, 0.0))
    return lhs.astype(bf16)


def to_lanes(tile):
    return jnp.concatenate([tile[k : k + 1] for k in range(tile.shape[0])], axis=1)


def to_tile(rows):
    line = rows[0:1] + rows[1:2]
    return jnp.concatenate(
        [line[:, 128 * k : 128 * (k + 1)] for k in range(line.shape[1] // 128)], axis=0
    )


def add_parts(ref):
    tile = ref[0].astype(f32)
    for k in range(1, ref.shape[0]):
        tile += ref[k].astype(f32)
    return tile


def spread(ref, tile):
    ref[...] = jnp.broadcast_to(tile.astype(ref.dtype)[None], ref.shape)


def by_core(core, own, other):
    return jnp.where(core == 0, own, other), jnp.where(core == 0, other, own)


def column_rows(scale, energy_t):
    return lax.dot_general(
        split_rows(to_lanes(scale)),
        energy_t,
        (((1,), (1,)), ((), ())),
        preferred_element_type=f32,
    )


def pack_kernel(core_ref, tower_ref, projection_ref, out_ref, tower, columns, sems):
    start = pl.multiple_of(core_ref[0] * 128, 128)
    copies = (
        pltpu.make_async_copy(tower_ref, tower, sems.at[0]),
        pltpu.make_async_copy(projection_ref.at[:, pl.ds(start, 128)], columns, sems.at[1]),
    )
    for copy in copies:
        copy.start()
    copies[1].wait()
    for k in range(16):
        out_ref[k, 64:, :] = columns[...]
    copies[0].wait()
    for k in range(16):
        out_ref[k, :64, :] = tower[:, ROWS * k : ROWS * (k + 1)]


def lists_kernel(half_ref, kept_ref, taken_ref, out_ref):
    half = half_ref[0]
    for lists_ref, index in ((kept_ref, half), (taken_ref, 1 - half)):
        rows = pl.ds(pl.multiple_of(512 * index, 512), 512)
        out_ref[rows, :] = rms_norm(lists_ref[...].astype(f32)).astype(bf16)


def hidden_kernel(core_ref, parts_ref, columns_ref, out_ref):
    contract = (((0,), (0,)), ((), ()))
    tower = parts_ref[:, :64, :].reshape(1024, ROWS)
    kept = parts_ref[:, 64:, :].reshape(1024, 128)
    taken = columns_ref[...].reshape(1024, 128)
    low, high = by_core(core_ref[0], kept, taken)
    hidden = lax.dot_general(
        tower, jnp.concatenate([low, high], axis=1), contract, preferred_element_type=f32
    )
    spread(out_ref, rms_norm(hidden))


def energy_blocks(points_ref, lists_ref, energy_ref):
    points = points_ref[...].reshape(8 * ROWS, DP)
    ones = split_rows(jnp.ones((1, 8 * ROWS), f32))
    tiles = []
    for k in range(4):
        rows = pl.ds(256 * k, 256)
        scores = lax.dot_general(
            lists_ref[rows, :], points, (((1,), (1,)), ((), ())), preferred_element_type=f32
        )
        block = jnp.exp2(scores * SLOPE - OFFSET).astype(bf16)
        energy_ref[rows, :] = block
        tiles.append(
            to_tile(
                lax.dot_general(ones, block, (((1,), (1,)), ((), ())), preferred_element_type=f32)
            )
        )
    return jnp.concatenate(tiles, axis=0)


def first_kernel(points_ref, lists_ref, energy_ref, column_ref):
    column_ref[...] = energy_blocks(points_ref, lists_ref, energy_ref)


def second_kernel(points_ref, lists_ref, first_ref, energy_ref, column_ref):
    spread(column_ref, first_ref[...] + energy_blocks(points_ref, lists_ref, energy_ref))


def row_kernel(core_ref, parts_ref, own_ref, other_ref, row_ref):
    lhs = split_rows(to_lanes(2.0 / add_parts(parts_ref)))
    own = to_tile(jnp.dot(lhs, own_ref[...], preferred_element_type=f32))
    other = to_tile(jnp.dot(lhs, other_ref[...], preferred_element_type=f32))
    spread(row_ref, jnp.concatenate(by_core(core_ref[0], own, other), axis=0))


def row_scales(core_ref, rows_ref):
    scale = 1.0 / add_parts(rows_ref)
    return by_core(core_ref[0], scale[:8], scale[8:])


def column_kernel(core_ref, rows_ref, own_ref, other_ref, column_ref):
    own, other = row_scales(core_ref, rows_ref)
    rows = column_rows(own, own_ref[...]) + column_rows(other, other_ref[...])
    spread(column_ref, to_tile(rows))


def down_lanes(row):
    return jnp.transpose(jnp.broadcast_to(row, (128, 128)))


def scaled_points(scale, points_ref):
    blocks = []
    for k in range(8):
        factor = down_lanes(scale[k : k + 1])
        block = points_ref[k].astype(f32) * jnp.concatenate([factor, factor], axis=1)
        blocks.append(block.astype(bf16))
    return jnp.concatenate(blocks, axis=0)


def update_kernel(
    core_ref, rows_ref, columns_ref, own_ref, other_ref, own_points, other_points, out_ref, log_ref
):
    own, other = row_scales(core_ref, rows_ref)
    log_ref[...] = jnp.log(own)
    col_scale = 2.0 / add_parts(columns_ref)
    own = scaled_points(own, own_points)
    other = scaled_points(other, other_points)
    for k in range(4):
        rows = pl.ds(256 * k, 256)
        sums = jnp.dot(own_ref[rows, :], own, preferred_element_type=f32)
        sums += jnp.dot(other_ref[rows, :], other, preferred_element_type=f32)
        for n in range(2):
            factor = down_lanes(col_scale[2 * k + n : 2 * k + n + 1])
            block = sums[128 * n : 128 * (n + 1)] * jnp.concatenate([factor, factor], axis=1)
            start = 4 * k + 2 * n
            out_ref[start : start + 2] = block.astype(bf16).reshape(2, 64, DP)


def finish_kernel(parts_ref, out_ref):
    out_ref[...] = rms_norm(add_parts(parts_ref))


def shape(dims, dtype):
    return jax.ShapeDtypeStruct(dims, dtype)


def on_device(tower_out, projection, centroids):
    half = lax.axis_index("yh")
    core = lax.axis_index("c")
    core_index = core.reshape(1)
    pairs = centroids.reshape(8, 2, 64, DP)
    kept = jnp.where(core == 0, pairs[:, 0], pairs[:, 1]).reshape(512, DP)
    taken = lax.ppermute(kept, "yh", SWAP)
    message = pl.pallas_call(
        pack_kernel,
        out_shape=shape((16, 128, 128), bf16),
        in_specs=[SCALAR] + [pl.BlockSpec(memory_space=pltpu.HBM)] * 2,
        out_specs=pl.BlockSpec(memory_space=VMEM),
        scratch_shapes=[
            VMEM((64, 2048), bf16),
            VMEM((64, 128), bf16),
            pltpu.SemaphoreType.DMA((2,)),
        ],
        compiler_params=LIMIT,
        name="pack",
    )(core_index, far(tower_out.T), far(projection))
    parts = lax.all_to_all(message, ("z", "yh"), 0, 0)
    parts, taken = lax.optimization_barrier((parts, taken))
    taken_columns = lax.ppermute(parts[:, 64:], "c", SWAP)
    unit_lists = call(lists_kernel, shape((1024, DP), bf16), "lists", 1, 2, cost=COST)(
        half.reshape(1), kept, taken
    )
    taken_columns, unit_lists = lax.optimization_barrier((taken_columns, unit_lists))
    gathered = call(hidden_kernel, shape((8, ROWS, DP), bf16), "hidden", 1, 2)(
        core_index, parts, taken_columns
    )
    points = lax.all_to_all(gathered, "z", 0, 0)
    other_points = lax.ppermute(points, "c", SWAP)

    energy_shape = VMEM((1024, 1024), bf16)
    own_energy, first = call(
        first_kernel, (energy_shape, shape((8, 128), f32)), "first_energy", 0, 2, cost=COST
    )(points, unit_lists)
    other_energy, columns = call(
        second_kernel, (energy_shape, shape((16, 8, 128), f32)), "second_energy", 0, 3, cost=COST
    )(other_points, unit_lists, first)

    for sweep in range(ITERS):
        last = sweep == ITERS - 1
        columns = lax.all_to_all(columns, CHIPS, 0, 0)
        rows = call(row_kernel, shape((16, 16, 128), f32 if last else bf16), "row_sums", 1, 3)(
            core_index, columns, stay(own_energy), stay(other_energy)
        )
        rows = lax.all_to_all(rows, LISTS, 0, 0)
        if not last:
            columns = call(column_kernel, shape((16, 8, 128), f32), "column_sums", 1, 3)(
                core_index, rows, stay(own_energy), stay(other_energy)
            )

    sums, row_log = call(
        update_kernel, (shape((16, 64, DP), bf16), shape((8, 128), f32)), "update", 1, 6
    )(core_index, rows, columns, stay(own_energy), stay(other_energy), points, other_points)
    owned = lax.all_to_all(sums, CHIPS, 0, 0)
    refreshed = call(finish_kernel, shape((64, DP), f32), "finish", 0, 1)(owned)

    taken_log = lax.ppermute(row_log, "yh", SWAP)
    low_log = jnp.where(half == 0, row_log, taken_log)
    high_log = jnp.where(half == 0, taken_log, row_log)
    row_log = jnp.stack([low_log, high_log], axis=1).reshape(16 * ROWS)
    return (refreshed, row_log)


def solution(mesh):
    fine = Mesh(mesh.devices.reshape(4, 2, 2, 8, 2), ("x", "yl", "c", "z", "yh"))
    pts, lst = ("x", "yl", "c"), ("z", "yh")
    return jax.shard_map(
        on_device,
        mesh=fine,
        in_specs=(P(pts, lst), P(lst, None), P(lst, None)),
        out_specs=(P(lst + pts, None), P(pts)),
        check_vma=False,
    )
```

```python
import math

import jax
import jax.numpy as jnp
from jax import lax
from jax.experimental import pallas as pl
from jax.experimental.pallas import tpu as pltpu
from jax.sharding import Mesh, PartitionSpec as P

DP = 256
ITERS = 3
ROWS = 128

temper = 0.05
SLOPE = math.log2(math.e) / (DP * temper)
OFFSET = math.log2(math.e) / temper
SWAP = [(0, 1), (1, 0)]
CHIPS = ("yh", "x", "yl")
LISTS = ("z", "c")
bf16 = jnp.bfloat16
f32 = jnp.float32
VMEM = pltpu.VMEM
SCALAR = pl.BlockSpec(memory_space=pltpu.SMEM)
LIMIT = pltpu.CompilerParams(vmem_limit_bytes=40 * 2**20)
COST = pl.CostEstimate(flops=2**29, bytes_accessed=2**22, transcendentals=2**20)


def whole(count):
    return [pl.BlockSpec(memory_space=VMEM)] * count


def stay(array):
    return pltpu.with_memory_space_constraint(array, VMEM)


def far(array):
    return pltpu.with_memory_space_constraint(array, pltpu.HBM)


def call(kernel, out_shape, name, scalars, count, scratch=(), cost=None):
    single = not isinstance(out_shape, tuple)
    return pl.pallas_call(
        kernel,
        out_shape=out_shape,
        in_specs=[SCALAR] * scalars + whole(count),
        out_specs=whole(1)[0] if single else whole(len(out_shape)),
        scratch_shapes=scratch,
        compiler_params=LIMIT,
        cost_estimate=cost,
        name=name,
    )


def rms_norm(values):
    return values * lax.rsqrt(jnp.mean(values * values, axis=-1, keepdims=True) + 1e-06)


def split_rows(row):
    high = row.astype(bf16).astype(f32)
    index = lax.broadcasted_iota(jnp.int32, (16, row.shape[1]), 0)
    lhs = jnp.where(index == 0, high, jnp.where(index == 1, row - high, 0.0))
    return lhs.astype(bf16)


def to_lanes(tile):
    return jnp.concatenate([tile[k : k + 1] for k in range(tile.shape[0])], axis=1)


def to_tile(rows):
    line = rows[0:1] + rows[1:2]
    return jnp.concatenate(
        [line[:, 128 * k : 128 * (k + 1)] for k in range(line.shape[1] // 128)], axis=0
    )


def add_parts(ref):
    tile = ref[0].astype(f32)
    for k in range(1, ref.shape[0]):
        tile += ref[k].astype(f32)
    return tile


def spread(ref, tile):
    ref[...] = jnp.broadcast_to(tile.astype(ref.dtype)[None], ref.shape)


def by_core(core, own, other):
    return jnp.where(core == 0, own, other), jnp.where(core == 0, other, own)


def column_rows(scale, energy_t):
    return lax.dot_general(
        split_rows(to_lanes(scale)),
        energy_t,
        (((1,), (1,)), ((), ())),
        preferred_element_type=f32,
    )


def pack_kernel(core_ref, tower_ref, projection_ref, out_ref, tower, columns, sems):
    start = pl.multiple_of(core_ref[0] * 128, 128)
    copies = (
        pltpu.make_async_copy(tower_ref, tower, sems.at[0]),
        pltpu.make_async_copy(projection_ref.at[:, pl.ds(start, 128)], columns, sems.at[1]),
    )
    for copy in copies:
        copy.start()
    copies[1].wait()
    for k in range(16):
        out_ref[k, 64:, :] = columns[...]
    copies[0].wait()
    for k in range(16):
        out_ref[k, :64, :] = tower[:, ROWS * k : ROWS * (k + 1)]


def lists_kernel(half_ref, kept_ref, taken_ref, out_ref):
    half = half_ref[0]
    for lists_ref, index in ((kept_ref, half), (taken_ref, 1 - half)):
        rows = pl.ds(pl.multiple_of(512 * index, 512), 512)
        out_ref[rows, :] = rms_norm(lists_ref[...].astype(f32)).astype(bf16)


def hidden_kernel(core_ref, parts_ref, columns_ref, out_ref):
    contract = (((0,), (0,)), ((), ()))
    tower = parts_ref[:, :64, :].reshape(1024, ROWS)
    kept = parts_ref[:, 64:, :].reshape(1024, 128)
    taken = columns_ref[...].reshape(1024, 128)
    low, high = by_core(core_ref[0], kept, taken)
    hidden = lax.dot_general(
        tower, jnp.concatenate([low, high], axis=1), contract, preferred_element_type=f32
    )
    spread(out_ref, rms_norm(hidden))


def energy_blocks(points_ref, lists_ref, energy_ref):
    points = points_ref[...].reshape(8 * ROWS, DP)
    ones = split_rows(jnp.ones((1, 8 * ROWS), f32))
    tiles = []
    for k in range(4):
        rows = pl.ds(256 * k, 256)
        scores = lax.dot_general(
            lists_ref[rows, :], points, (((1,), (1,)), ((), ())), preferred_element_type=f32
        )
        block = jnp.exp2(scores * SLOPE - OFFSET).astype(bf16)
        energy_ref[rows, :] = block
        tiles.append(
            to_tile(
                lax.dot_general(ones, block, (((1,), (1,)), ((), ())), preferred_element_type=f32)
            )
        )
    return jnp.concatenate(tiles, axis=0)


def first_kernel(points_ref, lists_ref, energy_ref, column_ref):
    column_ref[...] = energy_blocks(points_ref, lists_ref, energy_ref)


def second_kernel(points_ref, lists_ref, first_ref, energy_ref, column_ref):
    spread(column_ref, first_ref[...] + energy_blocks(points_ref, lists_ref, energy_ref))


def row_tile(core_ref, parts_ref, own_ref, other_ref):
    lhs = split_rows(to_lanes(2.0 / add_parts(parts_ref)))
    own = to_tile(jnp.dot(lhs, own_ref[...], preferred_element_type=f32))
    other = to_tile(jnp.dot(lhs, other_ref[...], preferred_element_type=f32))
    return jnp.concatenate(by_core(core_ref[0], own, other), axis=0)


def row_kernel(core_ref, parts_ref, own_ref, other_ref, row_ref):
    spread(row_ref, row_tile(core_ref, parts_ref, own_ref, other_ref))


def change_kernel(core_ref, parts_ref, own_ref, other_ref, sent_ref, row_ref):
    tile = row_tile(core_ref, parts_ref, own_ref, other_ref)
    spread(row_ref, tile - sent_ref[0].astype(f32))


def row_scales(core_ref, *rows):
    scale = 1.0 / sum(add_parts(rows_ref) for rows_ref in rows)
    return by_core(core_ref[0], scale[:8], scale[8:])


def column_kernel(core_ref, rows_ref, own_ref, other_ref, column_ref):
    own, other = row_scales(core_ref, rows_ref)
    rows = column_rows(own, own_ref[...]) + column_rows(other, other_ref[...])
    spread(column_ref, to_tile(rows))


def down_lanes(row):
    return jnp.transpose(jnp.broadcast_to(row, (128, 128)))


def scaled_points(scale, points_ref):
    blocks = []
    for k in range(8):
        factor = down_lanes(scale[k : k + 1])
        block = points_ref[k].astype(f32) * jnp.concatenate([factor, factor], axis=1)
        blocks.append(block.astype(bf16))
    return jnp.concatenate(blocks, axis=0)


def update_kernel(
    core_ref,
    rows_ref,
    change_ref,
    columns_ref,
    own_ref,
    other_ref,
    own_points,
    other_points,
    out_ref,
    log_ref,
):
    own, other = row_scales(core_ref, rows_ref, change_ref)
    log_ref[...] = jnp.log(own)
    col_scale = 2.0 / add_parts(columns_ref)
    own = scaled_points(own, own_points)
    other = scaled_points(other, other_points)
    for k in range(4):
        rows = pl.ds(256 * k, 256)
        sums = jnp.dot(own_ref[rows, :], own, preferred_element_type=f32)
        sums += jnp.dot(other_ref[rows, :], other, preferred_element_type=f32)
        for n in range(2):
            factor = down_lanes(col_scale[2 * k + n : 2 * k + n + 1])
            block = sums[128 * n : 128 * (n + 1)] * jnp.concatenate([factor, factor], axis=1)
            start = 4 * k + 2 * n
            out_ref[start : start + 2] = block.astype(bf16).reshape(2, 64, DP)


def finish_kernel(parts_ref, out_ref):
    out_ref[...] = rms_norm(add_parts(parts_ref))


def shape(dims, dtype):
    return jax.ShapeDtypeStruct(dims, dtype)


def on_device(tower_out, projection, centroids):
    half = lax.axis_index("yh")
    core = lax.axis_index("c")
    core_index = core.reshape(1)
    pairs = centroids.reshape(8, 2, 64, DP)
    kept = jnp.where(core == 0, pairs[:, 0], pairs[:, 1]).reshape(512, DP)
    taken = lax.ppermute(kept, "yh", SWAP)
    message = pl.pallas_call(
        pack_kernel,
        out_shape=shape((16, 128, 128), bf16),
        in_specs=[SCALAR] + [pl.BlockSpec(memory_space=pltpu.HBM)] * 2,
        out_specs=pl.BlockSpec(memory_space=VMEM),
        scratch_shapes=[
            VMEM((64, 2048), bf16),
            VMEM((64, 128), bf16),
            pltpu.SemaphoreType.DMA((2,)),
        ],
        compiler_params=LIMIT,
        name="pack",
    )(core_index, far(tower_out.T), far(projection))
    parts = lax.all_to_all(message, ("z", "yh"), 0, 0)
    parts, taken = lax.optimization_barrier((parts, taken))
    taken_columns = lax.ppermute(parts[:, 64:], "c", SWAP)
    unit_lists = call(lists_kernel, shape((1024, DP), bf16), "lists", 1, 2, cost=COST)(
        half.reshape(1), kept, taken
    )
    taken_columns, unit_lists = lax.optimization_barrier((taken_columns, unit_lists))
    gathered = call(hidden_kernel, shape((8, ROWS, DP), bf16), "hidden", 1, 2)(
        core_index, parts, taken_columns
    )
    points = lax.all_to_all(gathered, "z", 0, 0)
    other_points = lax.ppermute(points, "c", SWAP)

    energy_shape = VMEM((1024, 1024), bf16)
    own_energy, first = call(
        first_kernel, (energy_shape, shape((8, 128), f32)), "first_energy", 0, 2, cost=COST
    )(points, unit_lists)
    other_energy, columns = call(
        second_kernel, (energy_shape, shape((16, 8, 128), f32)), "second_energy", 0, 3, cost=COST
    )(other_points, unit_lists, first)

    sent_shape = shape((16, 16, 128), bf16)
    energies = (stay(own_energy), stay(other_energy))
    for sweep in range(ITERS - 1):
        columns = lax.all_to_all(columns, CHIPS, 0, 0)
        sent = call(row_kernel, sent_shape, "row_sums", 1, 3)(core_index, columns, *energies)
        rows = lax.all_to_all(sent, LISTS, 0, 0)
        columns = call(column_kernel, shape((16, 8, 128), f32), "column_sums", 1, 3)(
            core_index, rows, *energies
        )
    columns = lax.all_to_all(columns, CHIPS, 0, 0)
    change = call(change_kernel, sent_shape, "row_change", 1, 4)(
        core_index, columns, *energies, sent
    )
    change = lax.all_to_all(change, LISTS, 0, 0)

    sums, row_log = call(
        update_kernel, (shape((16, 64, DP), bf16), shape((8, 128), f32)), "update", 1, 7
    )(core_index, rows, change, columns, *energies, points, other_points)
    owned = lax.all_to_all(sums, CHIPS, 0, 0)
    refreshed = call(finish_kernel, shape((64, DP), f32), "finish", 0, 1)(owned)

    taken_log = lax.ppermute(row_log, "yh", SWAP)
    low_log = jnp.where(half == 0, row_log, taken_log)
    high_log = jnp.where(half == 0, taken_log, row_log)
    row_log = jnp.stack([low_log, high_log], axis=1).reshape(16 * ROWS)
    return (refreshed, row_log)


def solution(mesh):
    fine = Mesh(mesh.devices.reshape(4, 2, 2, 8, 2), ("x", "yl", "c", "z", "yh"))
    pts, lst = ("x", "yl", "c"), ("z", "yh")
    return jax.shard_map(
        on_device,
        mesh=fine,
        in_specs=(P(pts, lst), P(lst, None), P(lst, None)),
        out_specs=(P(lst + pts, None), P(pts)),
        check_vma=False,
    )
```

```python
import math

import jax
import jax.numpy as jnp
from jax import lax
from jax.experimental import pallas as pl
from jax.experimental.pallas import tpu as pltpu
from jax.sharding import Mesh, PartitionSpec as P

DP = 256
ITERS = 3
ROWS = 128

temper = 0.05
SLOPE = math.log2(math.e) / (DP * temper)
OFFSET = math.log2(math.e) / temper
SWAP = [(0, 1), (1, 0)]
CHIPS = ("yh", "x", "yl")
LISTS = ("c", "z")
bf16 = jnp.bfloat16
f32 = jnp.float32
VMEM = pltpu.VMEM
SCALAR = pl.BlockSpec(memory_space=pltpu.SMEM)
LIMIT = pltpu.CompilerParams(vmem_limit_bytes=40 * 2**20)
COST = pl.CostEstimate(flops=2**29, bytes_accessed=2**22, transcendentals=2**20)


def whole(count):
    return [pl.BlockSpec(memory_space=VMEM)] * count


def stay(array):
    return pltpu.with_memory_space_constraint(array, VMEM)


def far(array):
    return pltpu.with_memory_space_constraint(array, pltpu.HBM)


def call(kernel, out_shape, name, scalars, count, scratch=(), cost=None):
    single = not isinstance(out_shape, tuple)
    return pl.pallas_call(
        kernel,
        out_shape=out_shape,
        in_specs=[SCALAR] * scalars + whole(count),
        out_specs=whole(1)[0] if single else whole(len(out_shape)),
        scratch_shapes=scratch,
        compiler_params=LIMIT,
        cost_estimate=cost,
        name=name,
    )


def rms_norm(values):
    return values * lax.rsqrt(jnp.mean(values * values, axis=-1, keepdims=True) + 1e-06)


def split_rows(row):
    high = row.astype(bf16).astype(f32)
    index = lax.broadcasted_iota(jnp.int32, (16, row.shape[1]), 0)
    lhs = jnp.where(index == 0, high, jnp.where(index == 1, row - high, 0.0))
    return lhs.astype(bf16)


def to_lanes(tile):
    return jnp.concatenate([tile[k : k + 1] for k in range(tile.shape[0])], axis=1)


def to_tile(rows):
    line = rows[0:1] + rows[1:2]
    return jnp.concatenate(
        [line[:, 128 * k : 128 * (k + 1)] for k in range(line.shape[1] // 128)], axis=0
    )


def add_parts(ref):
    tile = ref[0].astype(f32)
    for k in range(1, ref.shape[0]):
        tile += ref[k].astype(f32)
    return tile


def spread(ref, tile):
    ref[...] = jnp.broadcast_to(tile.astype(ref.dtype)[None], ref.shape)


def by_core(core, own, other):
    return jnp.where(core == 0, own, other), jnp.where(core == 0, other, own)


def column_rows(scale, energy_t):
    return lax.dot_general(
        split_rows(to_lanes(scale)),
        energy_t,
        (((1,), (1,)), ((), ())),
        preferred_element_type=f32,
    )


def pack_kernel(core_ref, tower_ref, projection_ref, out_ref, tower, columns, sems):
    start = pl.multiple_of(core_ref[0] * 128, 128)
    copies = (
        pltpu.make_async_copy(tower_ref, tower, sems.at[0]),
        pltpu.make_async_copy(projection_ref.at[:, pl.ds(start, 128)], columns, sems.at[1]),
    )
    for copy in copies:
        copy.start()
    copies[1].wait()
    for k in range(16):
        out_ref[k, 64:, :] = columns[...]
    copies[0].wait()
    for k in range(16):
        out_ref[k, :64, :] = tower[:, ROWS * k : ROWS * (k + 1)]


def lists_kernel(half_ref, kept_ref, taken_ref, out_ref):
    half = half_ref[0]
    for lists_ref, index in ((kept_ref, half), (taken_ref, 1 - half)):
        rows = pl.ds(pl.multiple_of(512 * index, 512), 512)
        out_ref[rows, :] = rms_norm(lists_ref[...].astype(f32)).astype(bf16)


def hidden_kernel(core_ref, parts_ref, columns_ref, out_ref):
    contract = (((0,), (0,)), ((), ()))
    tower = parts_ref[:, :64, :].reshape(1024, ROWS)
    kept = parts_ref[:, 64:, :].reshape(1024, 128)
    taken = columns_ref[...].reshape(1024, 128)
    low, high = by_core(core_ref[0], kept, taken)
    hidden = lax.dot_general(
        tower, jnp.concatenate([low, high], axis=1), contract, preferred_element_type=f32
    )
    spread(out_ref, rms_norm(hidden))


def energy_blocks(points_ref, lists_ref, energy_ref):
    points = points_ref[...].reshape(8 * ROWS, DP)
    ones = split_rows(jnp.ones((1, 8 * ROWS), f32))
    tiles = []
    for k in range(4):
        rows = pl.ds(256 * k, 256)
        scores = lax.dot_general(
            lists_ref[rows, :], points, (((1,), (1,)), ((), ())), preferred_element_type=f32
        )
        block = jnp.exp2(scores * SLOPE - OFFSET).astype(bf16)
        energy_ref[rows, :] = block
        tiles.append(
            to_tile(
                lax.dot_general(ones, block, (((1,), (1,)), ((), ())), preferred_element_type=f32)
            )
        )
    return jnp.concatenate(tiles, axis=0)


def first_kernel(points_ref, lists_ref, energy_ref, column_ref):
    column_ref[...] = energy_blocks(points_ref, lists_ref, energy_ref)


def second_kernel(points_ref, lists_ref, first_ref, energy_ref, column_ref):
    spread(column_ref, first_ref[...] + energy_blocks(points_ref, lists_ref, energy_ref))


def row_tile(core_ref, parts_ref, own_ref, other_ref):
    lhs = split_rows(to_lanes(2.0 / add_parts(parts_ref)))
    own = to_tile(jnp.dot(lhs, own_ref[...], preferred_element_type=f32))
    other = to_tile(jnp.dot(lhs, other_ref[...], preferred_element_type=f32))
    return jnp.concatenate(by_core(core_ref[0], own, other), axis=0)


def row_kernel(core_ref, parts_ref, own_ref, other_ref, row_ref):
    spread(row_ref, row_tile(core_ref, parts_ref, own_ref, other_ref))


def change_kernel(core_ref, parts_ref, own_ref, other_ref, sent_ref, row_ref):
    tile = row_tile(core_ref, parts_ref, own_ref, other_ref)
    spread(row_ref, tile - sent_ref[0].astype(f32))


def row_scales(core_ref, *rows):
    scale = 1.0 / sum(add_parts(rows_ref) for rows_ref in rows)
    return by_core(core_ref[0], scale[:8], scale[8:])


def column_kernel(core_ref, rows_ref, own_ref, other_ref, column_ref):
    own, other = row_scales(core_ref, rows_ref)
    rows = column_rows(own, own_ref[...]) + column_rows(other, other_ref[...])
    spread(column_ref, to_tile(rows))


def down_lanes(row):
    return jnp.transpose(jnp.broadcast_to(row, (128, 128)))


def scaled_points(scale, points_ref):
    blocks = []
    for k in range(8):
        factor = down_lanes(scale[k : k + 1])
        block = points_ref[k].astype(f32) * jnp.concatenate([factor, factor], axis=1)
        blocks.append(block.astype(bf16))
    return jnp.concatenate(blocks, axis=0)


def update_kernel(
    core_ref,
    rows_ref,
    change_ref,
    columns_ref,
    own_ref,
    other_ref,
    own_points,
    other_points,
    out_ref,
    log_ref,
):
    own, other = row_scales(core_ref, rows_ref, change_ref)
    log_ref[...] = jnp.log(own)
    col_scale = 2.0 / add_parts(columns_ref)
    own = scaled_points(own, own_points)
    other = scaled_points(other, other_points)
    for k in range(4):
        rows = pl.ds(256 * k, 256)
        sums = jnp.dot(own_ref[rows, :], own, preferred_element_type=f32)
        sums += jnp.dot(other_ref[rows, :], other, preferred_element_type=f32)
        for n in range(2):
            factor = down_lanes(col_scale[2 * k + n : 2 * k + n + 1])
            block = sums[128 * n : 128 * (n + 1)] * jnp.concatenate([factor, factor], axis=1)
            start = 4 * k + 2 * n
            out_ref[start : start + 2] = block.astype(bf16).reshape(2, 64, DP)


def finish_kernel(parts_ref, out_ref):
    out_ref[...] = rms_norm(add_parts(parts_ref))


def shape(dims, dtype):
    return jax.ShapeDtypeStruct(dims, dtype)


def on_device(tower_out, projection, centroids):
    half = lax.axis_index("yh")
    core = lax.axis_index("c")
    core_index = core.reshape(1)
    pairs = centroids.reshape(8, 2, 64, DP)
    kept = jnp.where(core == 0, pairs[:, 0], pairs[:, 1]).reshape(512, DP)
    taken = lax.ppermute(kept, "yh", SWAP)
    message = pl.pallas_call(
        pack_kernel,
        out_shape=shape((16, 128, 128), bf16),
        in_specs=[SCALAR] + [pl.BlockSpec(memory_space=pltpu.HBM)] * 2,
        out_specs=pl.BlockSpec(memory_space=VMEM),
        scratch_shapes=[
            VMEM((64, 2048), bf16),
            VMEM((64, 128), bf16),
            pltpu.SemaphoreType.DMA((2,)),
        ],
        compiler_params=LIMIT,
        name="pack",
    )(core_index, far(tower_out.T), far(projection))
    parts = lax.all_to_all(message, ("z", "yh"), 0, 0)
    parts, taken = lax.optimization_barrier((parts, taken))
    taken_columns = lax.ppermute(parts[:, 64:], "c", SWAP)
    unit_lists = call(lists_kernel, shape((1024, DP), bf16), "lists", 1, 2, cost=COST)(
        half.reshape(1), kept, taken
    )
    taken_columns, unit_lists = lax.optimization_barrier((taken_columns, unit_lists))
    gathered = call(hidden_kernel, shape((8, ROWS, DP), bf16), "hidden", 1, 2)(
        core_index, parts, taken_columns
    )
    points = lax.all_to_all(gathered, "z", 0, 0)
    other_points = lax.ppermute(points, "c", SWAP)

    energy_shape = VMEM((1024, 1024), bf16)
    own_energy, first = call(
        first_kernel, (energy_shape, shape((8, 128), f32)), "first_energy", 0, 2, cost=COST
    )(points, unit_lists)
    other_energy, columns = call(
        second_kernel, (energy_shape, shape((16, 8, 128), f32)), "second_energy", 0, 3, cost=COST
    )(other_points, unit_lists, first)

    sent_shape = shape((16, 16, 128), bf16)
    energies = (stay(own_energy), stay(other_energy))
    for sweep in range(ITERS - 1):
        columns = lax.all_to_all(columns, CHIPS, 0, 0)
        sent = call(row_kernel, sent_shape, "row_sums", 1, 3)(core_index, columns, *energies)
        rows = lax.all_to_all(sent, LISTS, 0, 0)
        columns = call(column_kernel, shape((16, 8, 128), f32), "column_sums", 1, 3)(
            core_index, rows, *energies
        )
    columns = lax.all_to_all(columns, CHIPS, 0, 0)
    change = call(change_kernel, sent_shape, "row_change", 1, 4)(
        core_index, columns, *energies, sent
    )
    change = lax.all_to_all(change, LISTS, 0, 0)

    sums, row_log = call(
        update_kernel, (shape((16, 64, DP), bf16), shape((8, 128), f32)), "update", 1, 7
    )(core_index, rows, change, columns, *energies, points, other_points)
    owned = lax.all_to_all(sums, CHIPS, 0, 0)
    refreshed = call(finish_kernel, shape((64, DP), f32), "finish", 0, 1)(owned)

    taken_log = lax.ppermute(row_log, "yh", SWAP)
    low_log = jnp.where(half == 0, row_log, taken_log)
    high_log = jnp.where(half == 0, taken_log, row_log)
    row_log = jnp.stack([low_log, high_log], axis=1).reshape(16 * ROWS)
    return (refreshed, row_log)


def solution(mesh):
    fine = Mesh(mesh.devices.reshape(4, 2, 2, 8, 2), ("x", "yl", "c", "z", "yh"))
    pts, lst = ("x", "yl", "c"), ("z", "yh")
    return jax.shard_map(
        on_device,
        mesh=fine,
        in_specs=(P(pts, lst), P(lst, None), P(lst, None)),
        out_specs=(P(lst + pts, None), P(pts)),
        check_vma=False,
    )
```

```python
import math

import jax
import jax.numpy as jnp
from jax import lax
from jax.experimental import pallas as pl
from jax.experimental.pallas import tpu as pltpu
from jax.sharding import Mesh, PartitionSpec as P

DP = 256
ITERS = 3
ROWS = 128

temper = 0.05
SLOPE = math.log2(math.e) / (DP * temper)
OFFSET = math.log2(math.e) / temper
SWAP = [(0, 1), (1, 0)]
CHIPS = ("yh", "x", "yl")
LISTS = ("c", "z")
PLANE = ("yl", "yh", "x")
bf16 = jnp.bfloat16
f32 = jnp.float32
VMEM = pltpu.VMEM
SCALAR = pl.BlockSpec(memory_space=pltpu.SMEM)
LIMIT = pltpu.CompilerParams(vmem_limit_bytes=40 * 2**20)
COST = pl.CostEstimate(flops=2**29, bytes_accessed=2**22, transcendentals=2**20)


def whole(count):
    return [pl.BlockSpec(memory_space=VMEM)] * count


def stay(array):
    return pltpu.with_memory_space_constraint(array, VMEM)


def far(array):
    return pltpu.with_memory_space_constraint(array, pltpu.HBM)


def call(kernel, out_shape, name, scalars, count, scratch=(), cost=None):
    single = not isinstance(out_shape, tuple)
    return pl.pallas_call(
        kernel,
        out_shape=out_shape,
        in_specs=[SCALAR] * scalars + whole(count),
        out_specs=whole(1)[0] if single else whole(len(out_shape)),
        scratch_shapes=scratch,
        compiler_params=LIMIT,
        cost_estimate=cost,
        name=name,
    )


def rms_norm(values):
    return values * lax.rsqrt(jnp.mean(values * values, axis=-1, keepdims=True) + 1e-06)


def split_rows(row):
    high = row.astype(bf16).astype(f32)
    index = lax.broadcasted_iota(jnp.int32, (16, row.shape[1]), 0)
    lhs = jnp.where(index == 0, high, jnp.where(index == 1, row - high, 0.0))
    return lhs.astype(bf16)


def to_lanes(tile):
    return jnp.concatenate([tile[k : k + 1] for k in range(tile.shape[0])], axis=1)


def to_tile(rows):
    line = rows[0:1] + rows[1:2]
    return jnp.concatenate(
        [line[:, 128 * k : 128 * (k + 1)] for k in range(line.shape[1] // 128)], axis=0
    )


def add_parts(ref):
    tile = ref[0].astype(f32)
    for k in range(1, ref.shape[0]):
        tile += ref[k].astype(f32)
    return tile


def spread(ref, tile):
    ref[...] = jnp.broadcast_to(tile.astype(ref.dtype)[None], ref.shape)


def by_core(core, own, other):
    return jnp.where(core == 0, own, other), jnp.where(core == 0, other, own)


def column_rows(scale, energy_t):
    return lax.dot_general(
        split_rows(to_lanes(scale)),
        energy_t,
        (((1,), (1,)), ((), ())),
        preferred_element_type=f32,
    )


def pack_kernel(core_ref, tower_ref, projection_ref, out_ref, tower, columns, sems):
    start = pl.multiple_of(core_ref[0] * 128, 128)
    copies = (
        pltpu.make_async_copy(tower_ref, tower, sems.at[0]),
        pltpu.make_async_copy(projection_ref.at[:, pl.ds(start, 128)], columns, sems.at[1]),
    )
    for copy in copies:
        copy.start()
    copies[1].wait()
    for k in range(16):
        out_ref[k, 64:, :] = columns[...]
    copies[0].wait()
    for k in range(16):
        out_ref[k, :64, :] = tower[:, ROWS * k : ROWS * (k + 1)]


def lists_kernel(half_ref, kept_ref, taken_ref, out_ref):
    half = half_ref[0]
    for lists_ref, index in ((kept_ref, half), (taken_ref, 1 - half)):
        rows = pl.ds(pl.multiple_of(512 * index, 512), 512)
        out_ref[rows, :] = rms_norm(lists_ref[...].astype(f32)).astype(bf16)


def hidden_kernel(core_ref, parts_ref, columns_ref, out_ref):
    contract = (((0,), (0,)), ((), ()))
    tower = parts_ref[:, :64, :].reshape(1024, ROWS)
    kept = parts_ref[:, 64:, :].reshape(1024, 128)
    taken = columns_ref[...].reshape(1024, 128)
    low, high = by_core(core_ref[0], kept, taken)
    hidden = lax.dot_general(
        tower, jnp.concatenate([low, high], axis=1), contract, preferred_element_type=f32
    )
    spread(out_ref, rms_norm(hidden))


def energy_blocks(points_ref, lists_ref, energy_ref):
    points = points_ref[...].reshape(8 * ROWS, DP)
    ones = split_rows(jnp.ones((1, 8 * ROWS), f32))
    tiles = []
    for k in range(4):
        rows = pl.ds(256 * k, 256)
        scores = lax.dot_general(
            lists_ref[rows, :], points, (((1,), (1,)), ((), ())), preferred_element_type=f32
        )
        block = jnp.exp2(scores * SLOPE - OFFSET).astype(bf16)
        energy_ref[rows, :] = block
        tiles.append(
            to_tile(
                lax.dot_general(ones, block, (((1,), (1,)), ((), ())), preferred_element_type=f32)
            )
        )
    return jnp.concatenate(tiles, axis=0)


def first_kernel(points_ref, lists_ref, energy_ref, column_ref):
    column_ref[...] = energy_blocks(points_ref, lists_ref, energy_ref)


def second_kernel(points_ref, lists_ref, first_ref, energy_ref, column_ref):
    spread(column_ref, first_ref[...] + energy_blocks(points_ref, lists_ref, energy_ref))


def row_tile(core_ref, parts_ref, own_ref, other_ref):
    lhs = split_rows(to_lanes(2.0 / add_parts(parts_ref)))
    own = to_tile(jnp.dot(lhs, own_ref[...], preferred_element_type=f32))
    other = to_tile(jnp.dot(lhs, other_ref[...], preferred_element_type=f32))
    return jnp.concatenate(by_core(core_ref[0], own, other), axis=0)


def row_kernel(core_ref, parts_ref, own_ref, other_ref, row_ref):
    spread(row_ref, row_tile(core_ref, parts_ref, own_ref, other_ref))


def change_kernel(core_ref, parts_ref, own_ref, other_ref, sent_ref, row_ref):
    tile = row_tile(core_ref, parts_ref, own_ref, other_ref)
    spread(row_ref, tile - sent_ref[0].astype(f32))


def row_scales(core_ref, *rows):
    scale = 1.0 / sum(add_parts(rows_ref) for rows_ref in rows)
    return by_core(core_ref[0], scale[:8], scale[8:])


def column_kernel(core_ref, rows_ref, own_ref, other_ref, column_ref):
    own, other = row_scales(core_ref, rows_ref)
    rows = column_rows(own, own_ref[...]) + column_rows(other, other_ref[...])
    spread(column_ref, to_tile(rows))


def down_lanes(row):
    return jnp.transpose(jnp.broadcast_to(row, (128, 128)))


def scaled_points(scale, points_ref):
    blocks = []
    for k in range(8):
        factor = down_lanes(scale[k : k + 1])
        block = points_ref[k].astype(f32) * jnp.concatenate([factor, factor], axis=1)
        blocks.append(block.astype(bf16))
    return jnp.concatenate(blocks, axis=0)


def update_kernel(
    core_ref,
    rows_ref,
    change_ref,
    columns_ref,
    own_ref,
    other_ref,
    own_points,
    other_points,
    out_ref,
    log_ref,
):
    own, other = row_scales(core_ref, rows_ref, change_ref)
    log_ref[...] = jnp.log(own)
    col_scale = 2.0 / add_parts(columns_ref)
    own = scaled_points(own, own_points)
    other = scaled_points(other, other_points)
    for k in range(4):
        rows = pl.ds(256 * k, 256)
        sums = jnp.dot(own_ref[rows, :], own, preferred_element_type=f32)
        sums += jnp.dot(other_ref[rows, :], other, preferred_element_type=f32)
        for n in range(2):
            factor = down_lanes(col_scale[2 * k + n : 2 * k + n + 1])
            block = sums[128 * n : 128 * (n + 1)] * jnp.concatenate([factor, factor], axis=1)
            start = 4 * k + 2 * n
            out_ref[start : start + 2] = block.astype(bf16).reshape(2, 64, DP)


def finish_kernel(parts_ref, out_ref):
    out_ref[...] = rms_norm(add_parts(parts_ref))


def shape(dims, dtype):
    return jax.ShapeDtypeStruct(dims, dtype)


def on_device(tower_out, projection, centroids):
    half = lax.axis_index("yh")
    core = lax.axis_index("c")
    core_index = core.reshape(1)
    pairs = centroids.reshape(8, 2, 64, DP)
    kept = jnp.where(core == 0, pairs[:, 0], pairs[:, 1]).reshape(512, DP)
    taken = lax.ppermute(kept, "yh", SWAP)
    message = pl.pallas_call(
        pack_kernel,
        out_shape=shape((16, 128, 128), bf16),
        in_specs=[SCALAR] + [pl.BlockSpec(memory_space=pltpu.HBM)] * 2,
        out_specs=pl.BlockSpec(memory_space=VMEM),
        scratch_shapes=[
            VMEM((64, 2048), bf16),
            VMEM((64, 128), bf16),
            pltpu.SemaphoreType.DMA((2,)),
        ],
        compiler_params=LIMIT,
        name="pack",
    )(core_index, far(tower_out.T), far(projection))
    parts = lax.all_to_all(message, ("z", "yh"), 0, 0)
    parts, taken = lax.optimization_barrier((parts, taken))
    taken_columns = lax.ppermute(parts[:, 64:], "c", SWAP)
    unit_lists = call(lists_kernel, shape((1024, DP), bf16), "lists", 1, 2, cost=COST)(
        half.reshape(1), kept, taken
    )
    taken_columns, unit_lists = lax.optimization_barrier((taken_columns, unit_lists))
    gathered = call(hidden_kernel, shape((8, ROWS, DP), bf16), "hidden", 1, 2)(
        core_index, parts, taken_columns
    )
    points = lax.all_to_all(gathered, "z", 0, 0)
    other_points = lax.ppermute(points, "c", SWAP)

    energy_shape = VMEM((1024, 1024), bf16)
    own_energy, first = call(
        first_kernel, (energy_shape, shape((8, 128), f32)), "first_energy", 0, 2, cost=COST
    )(points, unit_lists)
    other_energy, columns = call(
        second_kernel, (energy_shape, shape((16, 8, 128), f32)), "second_energy", 0, 3, cost=COST
    )(other_points, unit_lists, first)

    sent_shape = shape((16, 16, 128), bf16)
    energies = (stay(own_energy), stay(other_energy))
    for sweep in range(ITERS - 1):
        columns = lax.all_to_all(columns, PLANE, 0, 0)
        sent = call(row_kernel, sent_shape, "row_sums", 1, 3)(core_index, columns, *energies)
        rows = lax.all_to_all(sent, LISTS, 0, 0)
        columns = call(column_kernel, shape((16, 8, 128), f32), "column_sums", 1, 3)(
            core_index, rows, *energies
        )
    columns = lax.all_to_all(columns, PLANE, 0, 0)
    change = call(change_kernel, sent_shape, "row_change", 1, 4)(
        core_index, columns, *energies, sent
    )
    change = lax.all_to_all(change, LISTS, 0, 0)

    sums, row_log = call(
        update_kernel, (shape((16, 64, DP), bf16), shape((8, 128), f32)), "update", 1, 7
    )(core_index, rows, change, columns, *energies, points, other_points)
    owned = lax.all_to_all(sums, CHIPS, 0, 0)
    refreshed = call(finish_kernel, shape((64, DP), f32), "finish", 0, 1)(owned)

    taken_log = lax.ppermute(row_log, "yh", SWAP)
    low_log = jnp.where(half == 0, row_log, taken_log)
    high_log = jnp.where(half == 0, taken_log, row_log)
    row_log = jnp.stack([low_log, high_log], axis=1).reshape(16 * ROWS)
    return (refreshed, row_log)


def solution(mesh):
    fine = Mesh(mesh.devices.reshape(4, 2, 2, 8, 2), ("x", "yl", "c", "z", "yh"))
    pts, lst = ("x", "yl", "c"), ("z", "yh")
    return jax.shard_map(
        on_device,
        mesh=fine,
        in_specs=(P(pts, lst), P(lst, None), P(lst, None)),
        out_specs=(P(lst + pts, None), P(pts)),
        check_vma=False,
    )
```
